256 devices in a mesh: leaf: 64 (over y_hi, z, x), rank: 4 (over y_lo, core).
Axes of the slice: x: 4, y: 4 (y_hi: 2, y_lo: 2; y = y_hi * 2 + y_lo), z: 8, core: 2. Of those that a mesh axis runs over, the one named last changes fastest.
Arguments:
- vectors: bfloat16 [4096, 64, 64], P('leaf'), may hold values from -6 to 6
- near_blocks: bfloat16 [4096, 32, 64, 64], P('leaf', 'rank'), may hold values from -0.125 to 0.125
- near_offsets: int32 [4096, 32], P('leaf', 'rank'), may hold values from -64 to 64
- near_count: int32 [4096], P('leaf'), may hold values from 1 to 32
- basis: bfloat16 [4096, 64, 64], P('leaf'), may hold values from -0.75 to 0.75
- child_transfer: bfloat16 [4096, 64, 64], P('leaf'), may hold values from -0.25 to 0.25
- parent_transfer: bfloat16 [512, 64, 64], P('leaf'), may hold values from -0.25 to 0.25
- leaf_coupling: bfloat16 [4096, 32, 64, 64], P('leaf', 'rank'), may hold values from -0.125 to 0.125
- leaf_offsets: int32 [4096, 32], P('leaf', 'rank'), may hold values from -64 to 64
- top_coupling: bfloat16 [64, 16, 64, 64], P('leaf', 'rank'), may hold values from -0.1875 to 0.1875
- top_ids: int32 [64, 16], P('leaf', 'rank'), may hold values from 0 to 63
Outputs:
- product: bfloat16 [4096, 64, 64], P('leaf', 'rank')
The draws below stay inside these ranges and needn't reach their ends.
All inputs are finite; a program needn't handle non-finite values.
Results may differ from the reference program's by a relative error of at most 0.015.
Values may be sent and summed in bfloat16 or wider, within the bound.
No kernel may reach another device: no remote copies, remote signals or barrier semaphores. Data moves between devices by JAX's collectives and lax.ppermute only.
A program may use at most 128 MiB of HBM per device.

```python
import jax
import jax.numpy as jnp
from jax import lax

P_SIZE = 64
R = 64
K = 64
NB = 32
IL = 32
TL = 16
LEAF_DEV = 64
LEAVES = 4096
NTOP = 64


def touch_ends(entries, key, least, high):
    spot = [jax.random.randint(jax.random.fold_in(key, axis), (), 0, length) for axis, length in enumerate(entries.shape)]
    longest = entries.shape.index(max(entries.shape))
    neighbour = spot[:longest] + [(spot[longest] + 1) % entries.shape[longest]] + spot[longest + 1:]
    return entries.at[tuple(spot)].set(least).at[tuple(neighbour)].set(high)


def level_of(key, shape, pieces, low, top_value):
    def one(position, blocks):
        steps = jax.random.uniform(jax.random.fold_in(jax.random.fold_in(key, 6), position), (blocks,), jnp.float32, low / len(pieces), top_value / len(pieces))
        return jnp.repeat(jnp.exp(steps), shape[position] // blocks).reshape((-1,) + (1,) * (len(shape) - position - 1))

    factor_of = one(*pieces[0])
    for cut in pieces[1:]:
        factor_of = factor_of * one(*cut)
    return factor_of


def scatter_about(key, shape, deviation, reach, cuts=(), kind=jnp.bfloat16):
    values = deviation * jax.random.normal(key, shape, jnp.float32)
    if cuts:
        values = values * level_of(key, shape, cuts, -0.22, 0.18)
    return jnp.clip(values, -reach, reach).astype(kind)


def setup_inputs(seed: int = 0) -> dict:
    splits = jax.random.split(jax.random.key(seed), 12)
    return {
        "vectors": scatter_about(splits[0], (LEAVES, P_SIZE, R), 1.0, 6.0, ((0, 64),)),
        "near_blocks": scatter_about(splits[1], (LEAVES, NB, P_SIZE, P_SIZE), (P_SIZE * NB) ** -0.5, 0.125, ((0, 64), (1, 4))),
        "near_offsets": touch_ends(jax.random.randint(splits[2], (LEAVES, NB), -LEAF_DEV, LEAF_DEV + 1), jax.random.fold_in(splits[2], 1), -LEAF_DEV, LEAF_DEV).astype(jnp.int32),
        "near_count": touch_ends(jax.random.randint(splits[3], (LEAVES,), 1, NB + 1), jax.random.fold_in(splits[3], 1), 1, NB).astype(jnp.int32),
        "basis": scatter_about(splits[4], (LEAVES, P_SIZE, K), P_SIZE ** -0.5, 0.75, ((0, 64),)),
        "child_transfer": scatter_about(splits[5], (LEAVES, K, K), (8 * K) ** -0.5, 0.25, ((0, 64),)),
        "parent_transfer": scatter_about(splits[6], (LEAVES // 8, K, K), (8 * K) ** -0.5, 0.25, ((0, 64),)),
        "leaf_coupling": scatter_about(splits[7], (LEAVES, IL, K, K), (K * IL) ** -0.5, 0.125, ((0, 64), (1, 4))),
        "leaf_offsets": touch_ends(jax.random.randint(splits[8], (LEAVES, IL), -LEAF_DEV, LEAF_DEV + 1), jax.random.fold_in(splits[8], 1), -LEAF_DEV, LEAF_DEV).astype(jnp.int32),
        "top_coupling": scatter_about(splits[9], (NTOP, TL, K, K), (K * TL) ** -0.5, 0.1875, ((0, 64), (1, 4))),
        "top_ids": touch_ends(jax.random.randint(splits[10], (NTOP, TL), 0, NTOP), jax.random.fold_in(splits[10], 1), 0, NTOP - 1).astype(jnp.int32),
    }


def reference(vectors, near_blocks, near_offsets, near_count, basis, child_transfer, parent_transfer, leaf_coupling, leaf_offsets, top_coupling, top_ids):
    highest = lax.Precision.HIGHEST
    leaf_ids = jnp.arange(LEAVES, dtype=jnp.int32)
    values = vectors.astype(jnp.float32)
    near_field = jnp.zeros((LEAVES, P_SIZE, R), jnp.float32)
    for slot in range(NB):
        source = jnp.clip(leaf_ids + near_offsets[:, slot], 0, LEAVES - 1).astype(jnp.int32)
        term = jnp.einsum("lpq,lqr->lpr", near_blocks[:, slot].astype(jnp.float32), values[source], precision=highest)
        live_slot = (slot < near_count)[:, None, None]
        near_field = near_field + jnp.where(live_slot, term, jnp.zeros_like(term))
    moments = jnp.einsum("lpk,lpr->lkr", basis.astype(jnp.float32), values, precision=highest).astype(jnp.bfloat16)
    middle = jnp.einsum("lkj,lkr->ljr", child_transfer.astype(jnp.float32), moments.astype(jnp.float32), precision=highest)
    middle = middle.reshape(LEAVES // 8, 8, K, R).sum(1).astype(jnp.bfloat16)
    upper = jnp.einsum("mkj,mkr->mjr", parent_transfer.astype(jnp.float32), middle.astype(jnp.float32), precision=highest)
    upper = upper.reshape(NTOP, 8, K, R).sum(1).astype(jnp.bfloat16)
    upper_f = upper.astype(jnp.float32)
    top_field = jnp.zeros((NTOP, K, R), jnp.float32)
    for slot in range(TL):
        top_field = top_field + jnp.einsum("tjk,tkr->tjr", top_coupling[:, slot].astype(jnp.float32), upper_f[top_ids[:, slot]], precision=highest)
    moments_f = moments.astype(jnp.float32)
    leaf_field = jnp.zeros((LEAVES, K, R), jnp.float32)
    for slot in range(IL):
        source = jnp.clip(leaf_ids + leaf_offsets[:, slot], 0, LEAVES - 1).astype(jnp.int32)
        leaf_field = leaf_field + jnp.einsum("ljk,lkr->ljr", leaf_coupling[:, slot].astype(jnp.float32), moments_f[source], precision=highest)
    middle_field = jnp.einsum("mjk,mkr->mjr", parent_transfer.astype(jnp.float32), jnp.repeat(top_field, 8, axis=0), precision=highest)
    local_field = leaf_field + jnp.einsum("ljk,lkr->ljr", child_transfer.astype(jnp.float32), jnp.repeat(middle_field, 8, axis=0), precision=highest)
    product = near_field + jnp.einsum("lpk,lkr->lpr", basis.astype(jnp.float32), local_field, precision=highest)
    return product.astype(jnp.bfloat16)
```

```python
import functools

import jax
import jax.numpy as jnp
from jax import lax
from jax.experimental import pallas as pl
from jax.experimental.pallas import tpu as pltpu
from jax.sharding import PartitionSpec as P

F32 = jnp.float32
BF16 = jnp.bfloat16
VMEM_LIMIT = 40 * 1024 * 1024
STEP = 8


def params():
    return pltpu.CompilerParams(vmem_limit_bytes=VMEM_LIMIT)


def dot(a, b):
    return jnp.dot(a, b, preferred_element_type=F32)


def dot_t(a, b):
    return lax.dot_general(a, b, (((0,), (0,)), ((), ())), preferred_element_type=F32)


def pack_kernel(v_ref, o_ref):
    half = o_ref.shape[0]
    o_ref[...] = jnp.concatenate([v_ref[:half], v_ref[half:]], axis=-1)


def pack(v):
    n, p, c = v.shape
    return pl.pallas_call(
        pack_kernel,
        out_shape=jax.ShapeDtypeStruct((n // 2, p, 2 * c), v.dtype),
        compiler_params=params(),
        name="pack_vectors",
    )(v)


def upward_kernel(v_ref, b_ref, c_ref, p_ref, mom_ref, up_ref, m_s, mid_s):
    n, k, c = m_s.shape
    half = n // 2
    for l in range(n):
        m_s[l] = dot_t(b_ref[l], v_ref[l]).astype(BF16)
    mom_ref[...] = jnp.concatenate([m_s[:half], m_s[half:]], axis=-1)
    for m in range(n // 8):
        child = c_ref[8 * m : 8 * m + 8].reshape(8 * k, k)
        mid_s[m] = dot_t(child, m_s[8 * m : 8 * m + 8].reshape(8 * k, c)).astype(BF16)
    up = dot_t(p_ref[...].reshape(8 * k, k), mid_s[...].reshape(8 * k, c)).astype(BF16)
    up_ref[...] = jnp.concatenate([up[: k // 2], up[k // 2 :]], axis=-1)


def upward(vectors, basis, child, parent):
    n, p, c = vectors.shape
    k = basis.shape[2]
    return pl.pallas_call(
        upward_kernel,
        out_shape=(
            jax.ShapeDtypeStruct((n // 2, k, 2 * c), BF16),
            jax.ShapeDtypeStruct((k // 2, 2 * c), BF16),
        ),
        scratch_shapes=[pltpu.VMEM((n, k, c), BF16), pltpu.VMEM((n // 8, k, c), BF16)],
        compiler_params=params(),
        name="upward",
    )(vectors, basis, child, parent)


def pairs_kernel(idx_ref, own_ref, a_ref, b_ref, blk_ref, out_ref, ext):
    step = pl.program_id(0)
    half = own_ref.shape[0]
    c = own_ref.shape[2] // 2
    slots = blk_ref.shape[1]

    @pl.when(step == 0)
    def _():
        for i, ref in enumerate((own_ref, a_ref, b_ref)):
            ext[2 * half * i : 2 * half * i + half] = ref[:, :, :c]
            ext[2 * half * i + half : 2 * half * (i + 1)] = ref[:, :, c:]
        ext[6 * half] = jnp.zeros(ext.shape[1:], BF16)

    for l in range(blk_ref.shape[0]):
        base = (step * blk_ref.shape[0] + l) * slots
        total = None
        for g in range(0, slots, 4):
            lhs = jnp.concatenate([blk_ref[l, g + j] for j in range(4)], axis=1)
            rhs = jnp.concatenate([ext[idx_ref[base + g + j]] for j in range(4)], axis=0)
            term = dot(lhs, rhs)
            total = term if total is None else total + term
        out_ref[l] = total


def pairs(idx, own, a, b, blocks, name):
    n, slots, p, q = blocks.shape
    half, k, c2 = own.shape
    whole = pl.BlockSpec((half, k, c2), lambda i, *_: (0, 0, 0))
    return pl.pallas_call(
        pairs_kernel,
        out_shape=jax.ShapeDtypeStruct((n, p, c2 // 2), F32),
        grid_spec=pltpu.PrefetchScalarGridSpec(
            num_scalar_prefetch=1,
            grid=(n // STEP,),
            in_specs=[
                whole,
                whole,
                whole,
                pl.BlockSpec((STEP, slots, p, q), lambda i, *_: (i, 0, 0, 0)),
            ],
            out_specs=pl.BlockSpec((STEP, p, c2 // 2), lambda i, *_: (i, 0, 0)),
            scratch_shapes=[pltpu.VMEM((6 * half + 1, k, c2 // 2), BF16)],
        ),
        compiler_params=params(),
        name=name,
    )(idx, own, a, b, blocks)


def join_kernel(
    s_ref, up_ref, coup_ref, par_ref, leaf_ref, near_ref, child_ref, basis_ref, send_ref, keep_ref, held, mid
):
    step = pl.program_id(0)
    core = s_ref[16]
    k = par_ref.shape[1]
    c = near_ref.shape[2]

    @pl.when(step == 0)
    def _():
        count = up_ref.shape[0]
        for i in range(count):
            held[i, : k // 2] = up_ref[i, :, :c]
            held[i, k // 2 :] = up_ref[i, :, c:]
        held[count] = jnp.zeros((k, c), BF16)
        top = None
        for g in range(0, coup_ref.shape[0], 4):
            lhs = jnp.concatenate([coup_ref[g + j] for j in range(4)], axis=1)
            rhs = jnp.concatenate([held[s_ref[g + j]] for j in range(4)], axis=0)
            term = dot(lhs, rhs)
            top = term if top is None else top + term
        top = top.astype(BF16)
        for m in range(par_ref.shape[0]):
            mid[m] = dot(par_ref[m], top).astype(BF16)

    rows = send_ref.shape[1]
    for l in range(near_ref.shape[0]):
        field = leaf_ref[l] + dot(child_ref[l], mid[step * near_ref.shape[0] // 8 + l // 8])
        part = (near_ref[l] + dot(basis_ref[l], field.astype(BF16))).astype(BF16)
        quarter = [part[rows * i : rows * (i + 1)] for i in range(4)]
        even = jnp.concatenate([quarter[0], quarter[2]], axis=1)
        odd = jnp.concatenate([quarter[1], quarter[3]], axis=1)
        keep_ref[l] = jnp.where(core == 0, even, odd)
        send_ref[l] = jnp.where(core == 0, odd, even)


def join(scalars, upper, coupling, parent, leaf_part, near_part, child, basis):
    n, p, c = near_part.shape
    k = parent.shape[1]
    full = lambda a: pl.BlockSpec(a.shape, lambda i, *_: (0,) * a.ndim)
    tile = lambda a: pl.BlockSpec((STEP,) + a.shape[1:], lambda i, *_: (i, 0, 0))
    out = jax.ShapeDtypeStruct((n, p // 4, 2 * c), BF16)
    return pl.pallas_call(
        join_kernel,
        out_shape=(out, out),
        grid_spec=pltpu.PrefetchScalarGridSpec(
            num_scalar_prefetch=1,
            grid=(n // STEP,),
            in_specs=[
                full(upper),
                full(coupling),
                full(parent),
                tile(leaf_part),
                tile(near_part),
                tile(child),
                tile(basis),
            ],
            out_specs=(tile(out), tile(out)),
            scratch_shapes=[
                pltpu.VMEM((upper.shape[0] + 1, k, c), BF16),
                pltpu.VMEM((parent.shape[0], k, c), BF16),
            ],
        ),
        compiler_params=params(),
        name="join",
    )(scalars, upper, coupling, parent, leaf_part, near_part, child, basis)


def half_kernel(s_ref, keep_ref, recv_ref, send_ref, own_ref):
    c = keep_ref.shape[2] // 2
    n = keep_ref.shape[0]
    low = s_ref[0] == 0
    total = keep_ref[...].astype(F32) + recv_ref[...].astype(F32)
    first, second = total[:, :, :c], total[:, :, c:]
    own_ref[...] = jnp.where(low, first, second)
    other = jnp.where(low, second, first).astype(BF16)
    send_ref[...] = jnp.concatenate([other[: n // 2], other[n // 2 :]], axis=-1)


def half_sum(scalars, keep, recv):
    n, rows, c2 = keep.shape
    return pl.pallas_call(
        half_kernel,
        out_shape=(
            jax.ShapeDtypeStruct((n // 2, rows, c2), BF16),
            jax.ShapeDtypeStruct((n, rows, c2 // 2), F32),
        ),
        in_specs=[pl.BlockSpec(memory_space=pltpu.SMEM), pl.BlockSpec(), pl.BlockSpec()],
        compiler_params=params(),
        name="half_sum",
    )(scalars, keep, recv)


def last_kernel(own_ref, recv_ref, out_ref):
    n = own_ref.shape[0]
    c = own_ref.shape[2]
    recv = recv_ref[...].astype(F32)
    out_ref[: n // 2] = (own_ref[: n // 2] + recv[:, :, :c]).astype(BF16)
    out_ref[n // 2 :] = (own_ref[n // 2 :] + recv[:, :, c:]).astype(BF16)


def last_sum(own, recv):
    return pl.pallas_call(
        last_kernel,
        out_shape=jax.ShapeDtypeStruct(own.shape, BF16),
        compiler_params=params(),
        name="last_sum",
    )(own, recv)


AXES = ("leaf", "rank")


def halo_pairs(leaves):
    out = []
    for leaf in range(leaves):
        for rank in range(4):
            to = leaf + 1 if rank & 1 else leaf - 1
            if 0 <= to < leaves:
                cross = 2 if {leaf, to} == {leaves // 2 - 1, leaves // 2} else 0
                out.append((leaf * 4 + rank, to * 4 + (rank ^ 1 ^ cross)))
    return out


def top_pairs(step):
    out = []
    for y_hi in range(2):
        for z in range(8):
            for x in range(4):
                for y_lo in range(2):
                    for core in range(2):
                        s = step(y_hi, z, x, y_lo, core)
                        source = (((s[0] * 8 + s[1] % 8) * 4 + s[2]) * 2 + s[3]) * 2 + s[4]
                        out.append((source, (((y_hi * 8 + z) * 4 + x) * 2 + y_lo) * 2 + core))
    return out


def collect_upper(upper):
    held = lax.ppermute(
        upper,
        AXES,
        top_pairs(lambda y_hi, z, x, y_lo, core: (y_hi ^ y_lo, z + core, x, 1 - y_lo, core)),
    )[None]
    for bit in (1, 2):
        got = lax.ppermute(
            held, AXES, top_pairs(lambda y_hi, z, x, y_lo, core: (y_hi, z, x ^ bit, y_lo, core))
        )
        held = jnp.concatenate([held, got], axis=0)
    for hop in (1, 2):
        got = lax.ppermute(
            held,
            AXES,
            top_pairs(lambda y_hi, z, x, y_lo, core: (y_hi, z + hop * (2 * core - 1), x, y_lo, core)),
        )
        held = jnp.concatenate([held, got], axis=0)
    return held


def shards(
    vectors,
    near_blocks,
    near_offsets,
    near_count,
    basis,
    child_transfer,
    parent_transfer,
    leaf_coupling,
    leaf_offsets,
    top_coupling,
    top_ids,
):
    leaf_dev, points, columns = vectors.shape
    leaves = lax.axis_size("leaf")
    total_leaves = leaf_dev * leaves
    leaf_pos = lax.axis_index("leaf")
    rank_pos = lax.axis_index("rank")
    core = rank_pos % 2
    y_lo = rank_pos // 2
    own_first = leaf_pos * leaf_dev
    ids = own_first + jnp.arange(leaf_dev, dtype=jnp.int32)
    slots = near_offsets.shape[1]

    def place(offsets):
        rel = jnp.clip(ids[:, None] + offsets, 0, total_leaves - 1) - own_first
        low = rel + jnp.where(core == 0, 2 * leaf_dev, 3 * leaf_dev)
        high = rel + jnp.where(core == 0, leaf_dev, 0)
        return jnp.where(rel < 0, low, jnp.where(rel >= leaf_dev, high, rel))

    slot_ids = rank_pos * slots + jnp.arange(slots, dtype=jnp.int32)
    near_idx = jnp.where(slot_ids[None, :] < near_count[:, None], place(near_offsets), 3 * leaf_dev)
    near_idx = near_idx.reshape(-1)
    leaf_idx = place(leaf_offsets).reshape(-1)

    route = halo_pairs(leaves)
    swap = [(i, i ^ 1) for i in range(4)]
    packed = pack(vectors)
    vec_a = lax.ppermute(packed, AXES, route)

    moments, upper = upward(vectors, basis, child_transfer, parent_transfer)
    mom_a = lax.ppermute(moments, AXES, route)

    k = parent_transfer.shape[1]
    tl = top_ids.shape[1]
    id_rows = jnp.pad(top_ids.astype(BF16), ((0, 15), (0, k - tl)))
    mixed = jnp.concatenate([top_coupling.reshape(tl * k, k), id_rows], axis=0)
    mixed = lax.all_gather(mixed, "rank", axis=0)
    coupling = mixed[:, : tl * k].reshape(4 * tl, k, k)
    all_ids = mixed[:, tl * k, :tl].reshape(-1).astype(jnp.int32)

    held = collect_upper(upper)
    y_hi, z, x = leaf_pos // 32, leaf_pos // 4 % 8, leaf_pos % 4
    turn = (2 * core - 1) * (all_ids // 4 % 8 - z - core) % 8
    here = (all_ids // 32 == (y_hi ^ y_lo)) & (turn < 4)
    position = jnp.where(here, turn * 4 + ((all_ids % 4) ^ x), 16)
    scalars = jnp.concatenate([position, core[None]]).astype(jnp.int32)

    vec_b = lax.ppermute(vec_a, "rank", swap)
    near_part = pairs(near_idx, packed, vec_a, vec_b, near_blocks, "near_pairs")
    mom_b = lax.ppermute(mom_a, "rank", swap)
    leaf_part = pairs(leaf_idx, moments, mom_a, mom_b, leaf_coupling, "leaf_pairs")

    send, keep = join(scalars, held, coupling, parent_transfer, leaf_part, near_part, child_transfer, basis)
    recv = lax.ppermute(send, "rank", swap)
    send, own = half_sum(y_lo[None].astype(jnp.int32), keep, recv)
    recv = lax.ppermute(send, "rank", [(i, i ^ 2) for i in range(4)])
    return last_sum(own, recv)


def solution(mesh):
    in_specs = (
        P("leaf", None, None),
        P("leaf", "rank", None, None),
        P("leaf", "rank"),
        P("leaf"),
        P("leaf", None, None),
        P("leaf", None, None),
        P("leaf", None, None),
        P("leaf", "rank", None, None),
        P("leaf", "rank"),
        P("leaf", "rank", None, None),
        P("leaf", "rank"),
    )
    out_specs = P("leaf", "rank", None)
    return jax.shard_map(shards, mesh=mesh, in_specs=in_specs, out_specs=out_specs, check_vma=False)
```

```python
import functools

import jax
import jax.numpy as jnp
from jax import lax
from jax.experimental import pallas as pl
from jax.experimental.pallas import tpu as pltpu
from jax.sharding import PartitionSpec as P

F32 = jnp.float32
BF16 = jnp.bfloat16
MIB = 1024 * 1024
VMEM = pl.BlockSpec(memory_space=pltpu.VMEM)
SMEM = pl.BlockSpec(memory_space=pltpu.SMEM)


def params(mib):
    return pltpu.CompilerParams(vmem_limit_bytes=mib * MIB)


def cost(us):
    return pl.CostEstimate(flops=0, bytes_accessed=int(us * 3.0e6), transcendentals=0)


def dot(a, b):
    return jnp.dot(a, b, preferred_element_type=F32)


def dot_t(a, b):
    return lax.dot_general(a, b, (((0,), (0,)), ((), ())), preferred_element_type=F32)


def pinned(*arrays):
    return [pltpu.with_memory_space_constraint(a, pltpu.HBM) for a in arrays]


def load(sources, targets, sems):
    copies = [pltpu.make_async_copy(a, b, sems.at[i]) for i, (a, b) in enumerate(zip(sources, targets))]
    for copy in copies:
        copy.start()
    return copies


def left_right(left, right):
    lane = lax.broadcasted_iota(jnp.int32, left.shape, left.ndim - 1)
    return jnp.where(lane < left.shape[-1] // 2, left, right)


def first_kernel(
    pos_ref, v_any, b_any, c_any, p_any, t_any, ids_any, near_any, count_any, leaf_any,
    out_ref, coup_ref, up_ref, near_idx, leaf_idx,
    v, b, c, p, t, ids, near, count, leaf, mid, sems, *, total,
):
    copies = load(
        (v_any, b_any, c_any, p_any, near_any, count_any, leaf_any, t_any, ids_any),
        (v, b, c, p, near, count, leaf, t, ids),
        sems,
    )
    n, _, k = b.shape
    cols = v.shape[2]
    half = n // 2
    copies[0].wait()
    out_ref[:half] = jnp.concatenate([v[:half], v[half:]], axis=-1)
    copies[1].wait()
    for i in range(half):
        both = dot_t(jnp.concatenate([b[i], b[half + i]], axis=1), out_ref[i])
        out_ref[half + i] = left_right(both[:k], both[k:]).astype(BF16)
    copies[2].wait()
    for m in range(n // 16):
        here = out_ref[half + 8 * m : half + 8 * m + 8].reshape(8 * k, 2 * cols)
        low = dot_t(c[8 * m : 8 * m + 8].reshape(8 * k, k), here)
        high = dot_t(c[half + 8 * m : half + 8 * m + 8].reshape(8 * k, k), here)
        mid[m] = left_right(low, high).astype(BF16)
    copies[3].wait()
    mids = n // 16
    here = mid[...].reshape(mids * k, 2 * cols)
    low = dot_t(p[:mids].reshape(mids * k, k), here)
    high = dot_t(p[mids:].reshape(mids * k, k), here)
    up = (low[:, :cols] + high[:, cols:]).astype(BF16)
    up_ref[...] = jnp.concatenate([up[: k // 2], up[k // 2 :]], axis=-1)

    slots = near.shape[0]
    own_first = pos_ref[0] * n
    rank = pos_ref[1]
    side = pos_ref[2]
    leaf_ids = own_first + lax.broadcasted_iota(jnp.int32, near.shape, 1)

    def place(offsets):
        rel = jnp.clip(leaf_ids + offsets, 0, total - 1) - own_first
        under = rel + jnp.where(side == 0, 2 * n, 3 * n)
        over = rel + jnp.where(side == 0, n, 0)
        return jnp.where(rel < 0, under, jnp.where(rel >= n, over, rel))

    slot = rank * slots + lax.broadcasted_iota(jnp.int32, near.shape, 0)
    for copy in copies[4:]:
        copy.wait()
    near_idx[...] = jnp.where(slot < count[...], place(near[...]), 3 * n)
    leaf_idx[...] = place(leaf[...])

    top_slots = t.shape[0] // 2
    coup_ref[:top_slots] = jnp.concatenate([t[:top_slots], t[top_slots:]], axis=-1)
    lane = lax.broadcasted_iota(jnp.int32, coup_ref.shape[1:], 1)
    row = jnp.zeros(coup_ref.shape[1:], F32)
    for s in range(2 * top_slots):
        row = jnp.where(lane == s, ids[0, s].astype(F32), row)
    coup_ref[top_slots] = row.astype(BF16)


def first(pos, ids, vectors, coupling, basis, child, parent, near_offsets, near_count, leaf_offsets, total):
    n, p, c = vectors.shape
    k = basis.shape[2]
    sources = (vectors, basis, child, parent, coupling)
    small = (ids, near_offsets, near_count, leaf_offsets)
    shape = near_offsets.shape
    return pl.pallas_call(
        functools.partial(first_kernel, total=total),
        out_shape=(
            jax.ShapeDtypeStruct((n, p, 2 * c), BF16),
            jax.ShapeDtypeStruct((coupling.shape[0] // 2 + 1, k, 2 * k), BF16),
            jax.ShapeDtypeStruct((k // 2, 2 * c), BF16),
            jax.ShapeDtypeStruct(shape, jnp.int32),
            jax.ShapeDtypeStruct(shape, jnp.int32),
        ),
        in_specs=[SMEM] + [pl.BlockSpec(memory_space=pltpu.HBM)] * 9,
        out_specs=(VMEM,) * 5,
        scratch_shapes=[pltpu.VMEM(a.shape, BF16) for a in sources]
        + [
            pltpu.SMEM(ids.shape, jnp.int32),
            pltpu.VMEM(shape, jnp.int32),
            pltpu.VMEM(near_count.shape, jnp.int32),
            pltpu.VMEM(shape, jnp.int32),
            pltpu.VMEM((n // 16, k, 2 * c), BF16),
            pltpu.SemaphoreType.DMA((9,)),
        ],
        compiler_params=params(16),
        cost_estimate=cost(3.0),
        name="first",
    )(pos, *pinned(*sources, *small))


CHUNK = 8
AHEAD = 3


def fields_kernel(
    near_idx, leaf_idx, own_ref, a_ref, b_ref, near_any, leaf_any, near_out, leaf_out, near, leaf, vec, mom, sems
):
    n, slots, p, k = near.shape
    chunks = n // CHUNK
    parts = []
    for i in range(chunks):
        rows = pl.ds(i * CHUNK, CHUNK)
        parts.append(
            [
                pltpu.make_async_copy(src.at[rows], dst.at[rows], sems.at[2 * i + j])
                for j, (src, dst) in enumerate(((near_any, near), (leaf_any, leaf)))
            ]
        )
    for i in range(AHEAD):
        for c in parts[i]:
            c.start()
    half = n // 2
    cols = own_ref.shape[2] // 2
    for i, ref in enumerate((own_ref, a_ref, b_ref)):
        for to, first in ((vec, 0), (mom, half)):
            to[n * i : n * i + half] = ref[first : first + half, :, :cols]
            to[n * i + half : n * (i + 1)] = ref[first : first + half, :, cols:]
    vec[3 * n] = jnp.zeros(vec.shape[1:], BF16)

    for i in range(chunks):
        for c in parts[i]:
            c.wait()
        if i + AHEAD < chunks:
            for c in parts[i + AHEAD]:
                c.start()
        for blocks, idx, store, out in ((near, near_idx, vec, near_out), (leaf, leaf_idx, mom, leaf_out)):
            for l in range(i * CHUNK, (i + 1) * CHUNK):
                total = None
                for g in range(0, slots, 4):
                    lhs = jnp.concatenate([blocks[l, g + j] for j in range(4)], axis=1)
                    rhs = jnp.concatenate([store[idx[g + j, l]] for j in range(4)], axis=0)
                    term = dot(lhs, rhs)
                    total = term if total is None else total + term
                out[l] = total


def fields(near_idx, leaf_idx, own, a, b, near, leaf):
    n, slots, p, k = near.shape
    c = own.shape[2] // 2
    out = jax.ShapeDtypeStruct((n, p, c), F32)
    return pl.pallas_call(
        fields_kernel,
        out_shape=(out, out),
        in_specs=[SMEM] * 2 + [VMEM] * 3 + [pl.BlockSpec(memory_space=pltpu.HBM)] * 2,
        out_specs=(VMEM, VMEM),
        scratch_shapes=[
            pltpu.VMEM(near.shape, BF16),
            pltpu.VMEM(leaf.shape, BF16),
            pltpu.VMEM((3 * n + 1, p, c), BF16),
            pltpu.VMEM((3 * n, k, c), BF16),
            pltpu.SemaphoreType.DMA((2 * n // CHUNK,)),
        ],
        compiler_params=params(26),
        cost_estimate=cost(8.0),
        name="fields",
    )(near_idx, leaf_idx, own, a, b, *pinned(near, leaf))


def join_kernel(
    pos_ref, up_ref, other_ref, coup0_ref, coup1_ref, coup2_ref, coup3_ref, par_ref, leaf_ref, near_ref, child_ref, basis_ref,
    send_ref, keep_ref, held, mid, where_v, where_s, sem,
):
    k = par_ref.shape[1]
    cols = near_ref.shape[2]
    half = up_ref.shape[0]
    count = 2 * half
    leaf_pos, rank = pos_ref[0], pos_ref[1]
    core = rank & 1
    blocks = (coup0_ref, coup1_ref, coup2_ref, coup3_ref)
    slots = coup0_ref.shape[0] - 1
    for r, block in enumerate(blocks):
        ids = block[slots, :16].astype(F32).astype(jnp.int32)[:8]
        dz = ((ids >> 2) & 7) ^ ((leaf_pos >> 2) & 7) ^ (4 * core)
        dx = (ids & 3) ^ (leaf_pos & 3)
        here = ((ids >> 5) == ((leaf_pos >> 5) ^ (rank >> 1))) & (dz < 4)
        where_v[r] = jnp.where(here, (dz & 1) + 2 * dx + 8 * (dz >> 1), count)
    copy = pltpu.make_async_copy(where_v, where_s, sem)
    copy.start()
    for start, ref in ((0, up_ref), (half, other_ref)):
        for i in range(half):
            held[start + i, : k // 2] = ref[i, :, :cols]
            held[start + i, k // 2 :] = ref[i, :, cols:]
    held[count] = jnp.zeros((k, cols), BF16)
    copy.wait()
    top = None
    for r, block in enumerate(blocks):
        lhs = jnp.concatenate([block[j] for j in range(slots)], axis=1)
        order = [j + slots * e for j in range(slots) for e in range(2)]
        rhs = jnp.concatenate([held[where_s[r, 0, o]] for o in order], axis=0)
        term = dot(lhs, rhs)
        top = term if top is None else top + term
    top = top.astype(BF16)
    for m in range(par_ref.shape[0]):
        mid[m] = dot(par_ref[m], top).astype(BF16)

    rows = send_ref.shape[1]
    for l in range(near_ref.shape[0]):
        field = leaf_ref[l] + dot(child_ref[l], mid[l // 8])
        part = (near_ref[l] + dot(basis_ref[l], field.astype(BF16))).astype(BF16)
        quarter = [part[rows * i : rows * (i + 1)] for i in range(4)]
        even = jnp.concatenate([quarter[0], quarter[2]], axis=1)
        odd = jnp.concatenate([quarter[1], quarter[3]], axis=1)
        keep_ref[l] = jnp.where(core == 0, even, odd)
        send_ref[l] = jnp.where(core == 0, odd, even)


def join(pos, upper, other, coupling, parent, leaf_part, near_part, child, basis):
    n, p, c = near_part.shape
    k = parent.shape[1]
    out = jax.ShapeDtypeStruct((n, p // 4, 2 * c), BF16)
    return pl.pallas_call(
        join_kernel,
        out_shape=(out, out),
        in_specs=[SMEM] + [VMEM] * 11,
        out_specs=(VMEM, VMEM),
        scratch_shapes=[
            pltpu.VMEM((2 * upper.shape[0] + 1, k, c), BF16),
            pltpu.VMEM((parent.shape[0], k, c), BF16),
            pltpu.VMEM((4, 8, 128), jnp.int32),
            pltpu.SMEM((4, 8, 128), jnp.int32),
            pltpu.SemaphoreType.DMA,
        ],
        compiler_params=params(8),
        cost_estimate=cost(2.0),
        name="join",
    )(pos, upper, other, *coupling, parent, leaf_part, near_part, child, basis)


def half_kernel(s_ref, keep_ref, recv_ref, send_ref, own_ref):
    c = keep_ref.shape[2] // 2
    n = keep_ref.shape[0]
    low = s_ref[0] == 0
    total = keep_ref[...].astype(F32) + recv_ref[...].astype(F32)
    first, second = total[:, :, :c], total[:, :, c:]
    own_ref[...] = jnp.where(low, first, second)
    other = jnp.where(low, second, first).astype(BF16)
    send_ref[...] = jnp.concatenate([other[: n // 2], other[n // 2 :]], axis=-1)


def half_sum(scalars, keep, recv):
    n, rows, c2 = keep.shape
    return pl.pallas_call(
        half_kernel,
        out_shape=(
            jax.ShapeDtypeStruct((n // 2, rows, c2), BF16),
            jax.ShapeDtypeStruct((n, rows, c2 // 2), F32),
        ),
        in_specs=[SMEM, VMEM, VMEM],
        out_specs=(VMEM, VMEM),
        compiler_params=params(8),
        cost_estimate=cost(0.3),
        name="half_sum",
    )(scalars, keep, recv)


def last_kernel(own_ref, recv_ref, out_ref):
    n = own_ref.shape[0]
    c = own_ref.shape[2]
    recv = recv_ref[...].astype(F32)
    out_ref[: n // 2] = (own_ref[: n // 2] + recv[:, :, :c]).astype(BF16)
    out_ref[n // 2 :] = (own_ref[n // 2 :] + recv[:, :, c:]).astype(BF16)


def last_sum(own, recv):
    return pl.pallas_call(
        last_kernel,
        out_shape=jax.ShapeDtypeStruct(own.shape, BF16),
        in_specs=[VMEM, VMEM],
        out_specs=VMEM,
        compiler_params=params(8),
        cost_estimate=cost(0.5),
        name="last_sum",
    )(own, recv)


AXES = ("leaf", "rank")


def halo_pairs(leaves):
    out = []
    for leaf in range(leaves):
        for rank in range(4):
            high = (rank & 1) != (leaf >= leaves // 2)
            to = leaf + 1 if high else leaf - 1
            if 0 <= to < leaves:
                cross = {leaf, to} == {leaves // 2 - 1, leaves // 2}
                out.append((leaf * 4 + rank, to * 4 + (rank ^ (2 if cross else 1))))
    return out


def top_pairs(step, cores):
    out = []
    for y_hi in range(2):
        for z in range(8):
            for x in range(4):
                for y_lo in range(2):
                    for core in cores:
                        s = step(y_hi, z, x, y_lo, core)
                        source = (((s[0] * 8 + s[1] % 8) * 4 + s[2]) * 2 + s[3]) * 2 + s[4]
                        out.append((source, (((y_hi * 8 + z) * 4 + x) * 2 + y_lo) * 2 + core))
    return out


def collect_upper(upper, coupling):
    def get(held, step):
        return lax.ppermute(held, AXES, top_pairs(step, (0, 1)))

    def x_step(bit):
        return lambda y_hi, z, x, y_lo, core: (y_hi, z, x ^ bit, y_lo, core)

    def z_step(bit):
        return lambda y_hi, z, x, y_lo, core: (y_hi, z ^ bit, x, y_lo, core)

    held = get(upper, lambda y_hi, z, x, y_lo, core: (y_hi ^ y_lo, z ^ (4 * core), x, y_lo, core))[None]
    held, coupling = lax.optimization_barrier((held, coupling))
    for step in (z_step(1), x_step(1), x_step(2)):
        held = jnp.concatenate([held, get(held, step)], axis=0)
    return coupling, held, get(held, z_step(2))


def shards(
    vectors,
    near_blocks,
    near_offsets,
    near_count,
    basis,
    child_transfer,
    parent_transfer,
    leaf_coupling,
    leaf_offsets,
    top_coupling,
    top_ids,
):
    leaf_dev, points, columns = vectors.shape
    leaves = lax.axis_size("leaf")
    total_leaves = leaf_dev * leaves
    leaf_pos = lax.axis_index("leaf")
    rank_pos = lax.axis_index("rank")
    core = rank_pos % 2
    y_lo = rank_pos // 2
    side = core ^ (leaf_pos >= leaves // 2)
    pos = jnp.stack([leaf_pos, rank_pos, side]).astype(jnp.int32)

    route = halo_pairs(leaves)
    swap = [(i, i ^ 1) for i in range(4)]
    own, coupling, upper, near_idx, leaf_idx = first(
        pos,
        top_ids,
        vectors,
        top_coupling[0],
        basis,
        child_transfer,
        parent_transfer,
        near_offsets.T,
        near_count[None],
        leaf_offsets.T,
        total_leaves,
    )
    halo_a = lax.ppermute(own, AXES, route)
    coupling = [coupling] + [
        lax.ppermute(coupling, "rank", [(i, i ^ bit) for i in range(4)]) for bit in (1, 2, 3)
    ]
    coupling, held, other = collect_upper(upper, coupling)
    halo_a, held = lax.optimization_barrier((halo_a, held))
    halo_b = lax.ppermute(halo_a, "rank", swap)
    near_part, leaf_part = fields(near_idx, leaf_idx, own, halo_a, halo_b, near_blocks, leaf_coupling)
    send, keep = join(
        pos, held, other, coupling, parent_transfer, leaf_part, near_part, child_transfer, basis
    )
    recv = lax.ppermute(send, "rank", swap)
    send, own = half_sum(y_lo[None].astype(jnp.int32), keep, recv)
    recv = lax.ppermute(send, "rank", [(i, i ^ 2) for i in range(4)])
    return last_sum(own, recv)


def solution(mesh):
    in_specs = (
        P("leaf", None, None),
        P("leaf", "rank", None, None),
        P("leaf", "rank"),
        P("leaf"),
        P("leaf", None, None),
        P("leaf", None, None),
        P("leaf", None, None),
        P("leaf", "rank", None, None),
        P("leaf", "rank"),
        P("leaf", "rank", None, None),
        P("leaf", "rank"),
    )
    out_specs = P("leaf", "rank", None)
    return jax.shard_map(shards, mesh=mesh, in_specs=in_specs, out_specs=out_specs, check_vma=False)
```

```python
import functools

import jax
import jax.numpy as jnp
from jax import lax
from jax.experimental import pallas as pl
from jax.experimental.pallas import tpu as pltpu
from jax.sharding import PartitionSpec as P

F32 = jnp.float32
BF16 = jnp.bfloat16
MIB = 1024 * 1024
VMEM = pl.BlockSpec(memory_space=pltpu.VMEM)
SMEM = pl.BlockSpec(memory_space=pltpu.SMEM)


def params(mib):
    return pltpu.CompilerParams(vmem_limit_bytes=mib * MIB)


def cost(us):
    return pl.CostEstimate(flops=0, bytes_accessed=int(us * 3.0e6), transcendentals=0)


def dot(a, b):
    return jnp.dot(a, b, preferred_element_type=F32)


def dot_t(a, b):
    return lax.dot_general(a, b, (((0,), (0,)), ((), ())), preferred_element_type=F32)


def pinned(*arrays):
    return [pltpu.with_memory_space_constraint(a, pltpu.HBM) for a in arrays]


def load(sources, targets, sems):
    copies = [pltpu.make_async_copy(a, b, sems.at[i]) for i, (a, b) in enumerate(zip(sources, targets))]
    for copy in copies:
        copy.start()
    return copies


def left_right(left, right):
    lane = lax.broadcasted_iota(jnp.int32, left.shape, left.ndim - 1)
    return jnp.where(lane < left.shape[-1] // 2, left, right)


def first_kernel(
    pos_ref, v_any, b_any, c_any, p_any, near_any, count_any, leaf_any, t_any, ids_any,
    out_ref, up_ref, near_idx, leaf_idx, c0_ref, c1_ref, c2_ref, c3_ref,
    v, b, c, p, near, count, leaf, t, ids, mid, sems, *, total,
):
    copies = load(
        (v_any, b_any, c_any, p_any, near_any, count_any, leaf_any, t_any, ids_any),
        (v, b, c, p, near, count, leaf, t, ids),
        sems,
    )
    n, _, k = b.shape
    cols = v.shape[2]
    half = n // 2
    copies[0].wait()
    out_ref[:half] = jnp.concatenate([v[:half], v[half:]], axis=-1)
    copies[1].wait()
    for i in range(half):
        both = dot_t(jnp.concatenate([b[i], b[half + i]], axis=1), out_ref[i])
        out_ref[half + i] = left_right(both[:k], both[k:]).astype(BF16)
    copies[2].wait()
    for m in range(n // 16):
        here = out_ref[half + 8 * m : half + 8 * m + 8].reshape(8 * k, 2 * cols)
        low = dot_t(c[8 * m : 8 * m + 8].reshape(8 * k, k), here)
        high = dot_t(c[half + 8 * m : half + 8 * m + 8].reshape(8 * k, k), here)
        mid[m] = left_right(low, high).astype(BF16)
    copies[3].wait()
    mids = n // 16
    here = mid[...].reshape(mids * k, 2 * cols)
    low = dot_t(p[:mids].reshape(mids * k, k), here)
    high = dot_t(p[mids:].reshape(mids * k, k), here)
    up = low[:, :cols] + high[:, cols:]
    rank = pos_ref[1]
    piece = k // 4
    quarter = up[:piece]
    for r in range(1, 4):
        quarter = jnp.where(rank == r, up[piece * r : piece * (r + 1)], quarter)
    quarter = jnp.concatenate([quarter[: piece // 2], quarter[piece // 2 :]], axis=-1).astype(BF16)
    for i in range(up_ref.shape[0]):
        up_ref[i] = quarter

    slots = near.shape[0]
    own_first = pos_ref[0] * n
    side = pos_ref[2]
    leaf_ids = own_first + lax.broadcasted_iota(jnp.int32, near.shape, 1)

    def place(offsets):
        rel = jnp.clip(leaf_ids + offsets, 0, total - 1) - own_first
        under = rel + jnp.where(side == 0, 2 * n, 3 * n)
        over = rel + jnp.where(side == 0, n, 0)
        return jnp.where(rel < 0, under, jnp.where(rel >= n, over, rel))

    slot = rank * slots + lax.broadcasted_iota(jnp.int32, near.shape, 0)
    for copy in copies[4:]:
        copy.wait()
    near_idx[...] = jnp.where(slot < count[...], place(near[...]), 3 * n)
    leaf_idx[...] = place(leaf[...])

    top_slots = t.shape[0]
    columns = []
    for r in range(4):
        part = jnp.concatenate([t[s, :, piece * r : piece * (r + 1)] for s in range(top_slots)], axis=1)
        columns.append(jnp.concatenate([part[: k // 2], part[k // 2 :]], axis=1))
    lane = lax.broadcasted_iota(jnp.int32, (16, 2 * k), 1)
    row = jnp.zeros((16, 2 * k), F32)
    for s in range(top_slots):
        row = jnp.where(lane == s, ids[0, s].astype(F32), row)
    for bit, ref in enumerate((c0_ref, c1_ref, c2_ref, c3_ref)):
        to = rank ^ bit
        part = columns[0]
        for r in range(1, 4):
            part = jnp.where(to == r, columns[r], part)
        ref[: k // 2] = part
        ref[k // 2 :] = row.astype(BF16)


def first(pos, vectors, basis, child, parent, near_offsets, near_count, leaf_offsets, coupling, ids, total):
    n, p, c = vectors.shape
    k = basis.shape[2]
    sources = (vectors, basis, child, parent)
    small = (near_offsets, near_count, leaf_offsets)
    shape = near_offsets.shape
    return pl.pallas_call(
        functools.partial(first_kernel, total=total),
        out_shape=(
            jax.ShapeDtypeStruct((n, p, 2 * c), BF16),
            jax.ShapeDtypeStruct((total // n, k // 8, 2 * c), BF16),
            jax.ShapeDtypeStruct(shape, jnp.int32),
            jax.ShapeDtypeStruct(shape, jnp.int32),
        )
        + (jax.ShapeDtypeStruct((k // 2 + 16, 2 * k), BF16),) * 4,
        in_specs=[SMEM] + [pl.BlockSpec(memory_space=pltpu.HBM)] * 9,
        out_specs=(VMEM,) * 8,
        scratch_shapes=[pltpu.VMEM(a.shape, BF16) for a in sources]
        + [
            pltpu.VMEM(shape, jnp.int32),
            pltpu.VMEM(near_count.shape, jnp.int32),
            pltpu.VMEM(shape, jnp.int32),
            pltpu.VMEM(coupling.shape, BF16),
            pltpu.SMEM(ids.shape, jnp.int32),
            pltpu.VMEM((n // 16, k, 2 * c), BF16),
            pltpu.SemaphoreType.DMA((9,)),
        ],
        compiler_params=params(16),
        cost_estimate=cost(3.0),
        name="first",
    )(pos, *pinned(*sources, *small, coupling, ids))


CHUNK = 8
AHEAD = 3


def fields_kernel(
    near_idx, leaf_idx, own_ref, a_ref, b_ref, near_any, leaf_any, near_out, leaf_out, near, leaf, vec, mom, sems
):
    n, slots, p, k = near.shape
    chunks = n // CHUNK
    parts = []
    for i in range(chunks):
        rows = pl.ds(i * CHUNK, CHUNK)
        parts.append(
            [
                pltpu.make_async_copy(src.at[rows], dst.at[rows], sems.at[2 * i + j])
                for j, (src, dst) in enumerate(((near_any, near), (leaf_any, leaf)))
            ]
        )
    for i in range(AHEAD):
        for c in parts[i]:
            c.start()
    half = n // 2
    cols = own_ref.shape[2] // 2
    for i, ref in enumerate((own_ref, a_ref, b_ref)):
        for to, first in ((vec, 0), (mom, half)):
            to[n * i : n * i + half] = ref[first : first + half, :, :cols]
            to[n * i + half : n * (i + 1)] = ref[first : first + half, :, cols:]
    vec[3 * n] = jnp.zeros(vec.shape[1:], BF16)

    for i in range(chunks):
        for c in parts[i]:
            c.wait()
        if i + AHEAD < chunks:
            for c in parts[i + AHEAD]:
                c.start()
        for blocks, idx, store, out in ((near, near_idx, vec, near_out), (leaf, leaf_idx, mom, leaf_out)):
            for l in range(i * CHUNK, (i + 1) * CHUNK):
                total = None
                for g in range(0, slots, 4):
                    lhs = jnp.concatenate([blocks[l, g + j] for j in range(4)], axis=1)
                    rhs = jnp.concatenate([store[idx[g + j, l]] for j in range(4)], axis=0)
                    term = dot(lhs, rhs)
                    total = term if total is None else total + term
                out[l] = total


def fields(near_idx, leaf_idx, own, a, b, near, leaf):
    n, slots, p, k = near.shape
    c = own.shape[2] // 2
    out = jax.ShapeDtypeStruct((n, p, c), F32)
    return pl.pallas_call(
        fields_kernel,
        out_shape=(out, out),
        in_specs=[SMEM] * 2 + [VMEM] * 3 + [pl.BlockSpec(memory_space=pltpu.HBM)] * 2,
        out_specs=(VMEM, VMEM),
        scratch_shapes=[
            pltpu.VMEM(near.shape, BF16),
            pltpu.VMEM(leaf.shape, BF16),
            pltpu.VMEM((3 * n + 1, p, c), BF16),
            pltpu.VMEM((3 * n, k, c), BF16),
            pltpu.SemaphoreType.DMA((2 * n // CHUNK,)),
        ],
        compiler_params=params(26),
        cost_estimate=cost(8.0),
        name="fields",
    )(near_idx, leaf_idx, own, a, b, *pinned(near, leaf))


def join_kernel(
    pos_ref, up_ref, c0_ref, c1_ref, c2_ref, c3_ref, par_ref, leaf_ref, near_ref, child_ref, basis_ref,
    send_ref, keep_ref, mid, ids_v, ids_s, sem,
):
    cols = near_ref.shape[2]
    k = par_ref.shape[1]
    core = pos_ref[1] & 1
    parts = (c0_ref, c1_ref, c2_ref, c3_ref)
    for b, ref in enumerate(parts):
        ids_v[b] = ref[k // 2 :].astype(F32).astype(jnp.int32)[:8]
    copy = pltpu.make_async_copy(ids_v, ids_s, sem)
    copy.start()
    lhs = [ref[: k // 2] for ref in parts]
    lhs = jnp.concatenate([jnp.concatenate([c[:, :k], c[:, k:]], axis=0) for c in lhs], axis=1)
    copy.wait()
    rhs = []
    for b in range(4):
        for s in range(4):
            u = up_ref[ids_s[b, 0, s]].astype(F32)
            rhs += [u[:, :cols], u[:, cols:]]
    top = dot(lhs, jnp.concatenate(rhs, axis=0).astype(BF16))
    top = top.astype(BF16)
    for m in range(par_ref.shape[0]):
        mid[m] = dot(par_ref[m], top).astype(BF16)

    rows = send_ref.shape[1]
    for l in range(near_ref.shape[0]):
        field = leaf_ref[l] + dot(child_ref[l], mid[l // 8])
        part = (near_ref[l] + dot(basis_ref[l], field.astype(BF16))).astype(BF16)
        quarter = [part[rows * i : rows * (i + 1)] for i in range(4)]
        even = jnp.concatenate([quarter[0], quarter[2]], axis=1)
        odd = jnp.concatenate([quarter[1], quarter[3]], axis=1)
        keep_ref[l] = jnp.where(core == 0, even, odd)
        send_ref[l] = jnp.where(core == 0, odd, even)


def join(pos, upper, coupling, parent, leaf_part, near_part, child, basis):
    n, p, c = near_part.shape
    k = parent.shape[1]
    out = jax.ShapeDtypeStruct((n, p // 4, 2 * c), BF16)
    return pl.pallas_call(
        join_kernel,
        out_shape=(out, out),
        in_specs=[SMEM] + [VMEM] * 10,
        out_specs=(VMEM, VMEM),
        scratch_shapes=[
            pltpu.VMEM((parent.shape[0], k, c), BF16),
            pltpu.VMEM((4, 8, 2 * k), jnp.int32),
            pltpu.SMEM((4, 8, 2 * k), jnp.int32),
            pltpu.SemaphoreType.DMA,
        ],
        compiler_params=params(8),
        cost_estimate=cost(2.0),
        name="join",
    )(pos, upper, *coupling, parent, leaf_part, near_part, child, basis)


def half_kernel(s_ref, keep_ref, recv_ref, send_ref, own_ref):
    c = keep_ref.shape[2] // 2
    n = keep_ref.shape[0]
    low = s_ref[0] == 0
    total = keep_ref[...].astype(F32) + recv_ref[...].astype(F32)
    first, second = total[:, :, :c], total[:, :, c:]
    own_ref[...] = jnp.where(low, first, second)
    other = jnp.where(low, second, first).astype(BF16)
    send_ref[...] = jnp.concatenate([other[: n // 2], other[n // 2 :]], axis=-1)


def half_sum(scalars, keep, recv):
    n, rows, c2 = keep.shape
    return pl.pallas_call(
        half_kernel,
        out_shape=(
            jax.ShapeDtypeStruct((n // 2, rows, c2), BF16),
            jax.ShapeDtypeStruct((n, rows, c2 // 2), F32),
        ),
        in_specs=[SMEM, VMEM, VMEM],
        out_specs=(VMEM, VMEM),
        compiler_params=params(8),
        cost_estimate=cost(0.3),
        name="half_sum",
    )(scalars, keep, recv)


def last_kernel(own_ref, recv_ref, out_ref):
    n = own_ref.shape[0]
    c = own_ref.shape[2]
    recv = recv_ref[...].astype(F32)
    out_ref[: n // 2] = (own_ref[: n // 2] + recv[:, :, :c]).astype(BF16)
    out_ref[n // 2 :] = (own_ref[n // 2 :] + recv[:, :, c:]).astype(BF16)


def last_sum(own, recv):
    return pl.pallas_call(
        last_kernel,
        out_shape=jax.ShapeDtypeStruct(own.shape, BF16),
        in_specs=[VMEM, VMEM],
        out_specs=VMEM,
        compiler_params=params(8),
        cost_estimate=cost(0.5),
        name="last_sum",
    )(own, recv)


AXES = ("leaf", "rank")


def halo_pairs(leaves):
    out = []
    for leaf in range(leaves):
        for rank in range(4):
            high = (rank & 1) != (leaf >= leaves // 2)
            to = leaf + 1 if high else leaf - 1
            if 0 <= to < leaves:
                cross = {leaf, to} == {leaves // 2 - 1, leaves // 2}
                out.append((leaf * 4 + rank, to * 4 + (rank ^ (2 if cross else 1))))
    return out


def shards(
    vectors,
    near_blocks,
    near_offsets,
    near_count,
    basis,
    child_transfer,
    parent_transfer,
    leaf_coupling,
    leaf_offsets,
    top_coupling,
    top_ids,
):
    leaf_dev, points, columns = vectors.shape
    leaves = lax.axis_size("leaf")
    total_leaves = leaf_dev * leaves
    leaf_pos = lax.axis_index("leaf")
    rank_pos = lax.axis_index("rank")
    core = rank_pos % 2
    y_lo = rank_pos // 2
    side = core ^ (leaf_pos >= leaves // 2)
    pos = jnp.stack([leaf_pos, rank_pos, side]).astype(jnp.int32)

    route = halo_pairs(leaves)
    swap = [(i, i ^ 1) for i in range(4)]
    own, upper, near_idx, leaf_idx, *coupling = first(
        pos,
        vectors,
        basis,
        child_transfer,
        parent_transfer,
        near_offsets.T,
        near_count[None],
        leaf_offsets.T,
        top_coupling[0],
        top_ids,
        total_leaves,
    )
    halo_a = lax.ppermute(own, AXES, route)
    upper = lax.all_to_all(upper, "leaf", 0, 0)
    halo_a, upper, coupling = lax.optimization_barrier((halo_a, upper, coupling))
    halo_b = lax.ppermute(halo_a, "rank", swap)
    coupling = coupling[:1] + [
        lax.ppermute(coupling[bit], "rank", [(i, i ^ bit) for i in range(4)]) for bit in (1, 2, 3)
    ]
    near_part, leaf_part = fields(near_idx, leaf_idx, own, halo_a, halo_b, near_blocks, leaf_coupling)
    send, keep = join(
        pos, upper, coupling, parent_transfer, leaf_part, near_part, child_transfer, basis
    )
    recv = lax.ppermute(send, "rank", swap)
    send, own = half_sum(y_lo[None].astype(jnp.int32), keep, recv)
    recv = lax.ppermute(send, "rank", [(i, i ^ 2) for i in range(4)])
    return last_sum(own, recv)


def solution(mesh):
    in_specs = (
        P("leaf", None, None),
        P("leaf", "rank", None, None),
        P("leaf", "rank"),
        P("leaf"),
        P("leaf", None, None),
        P("leaf", None, None),
        P("leaf", None, None),
        P("leaf", "rank", None, None),
        P("leaf", "rank"),
        P("leaf", "rank", None, None),
        P("leaf", "rank"),
    )
    out_specs = P("leaf", "rank", None)
    return jax.shard_map(shards, mesh=mesh, in_specs=in_specs, out_specs=out_specs, check_vma=False)
```

```python
import functools

import jax
import jax.numpy as jnp
from jax import lax
from jax.experimental import pallas as pl
from jax.experimental.pallas import tpu as pltpu
from jax.sharding import PartitionSpec as P

F32 = jnp.float32
BF16 = jnp.bfloat16
MIB = 1024 * 1024
VMEM = pl.BlockSpec(memory_space=pltpu.VMEM)
SMEM = pl.BlockSpec(memory_space=pltpu.SMEM)


def params(mib):
    return pltpu.CompilerParams(vmem_limit_bytes=mib * MIB)


def cost(us):
    return pl.CostEstimate(flops=0, bytes_accessed=int(us * 3.0e6), transcendentals=0)


def dot(a, b):
    return jnp.dot(a, b, preferred_element_type=F32)


def dot_t(a, b):
    return lax.dot_general(a, b, (((0,), (0,)), ((), ())), preferred_element_type=F32)


def pinned(*arrays):
    return [pltpu.with_memory_space_constraint(a, pltpu.HBM) for a in arrays]


def load(sources, targets, sems):
    copies = [pltpu.make_async_copy(a, b, sems.at[i]) for i, (a, b) in enumerate(zip(sources, targets))]
    for copy in copies:
        copy.start()
    return copies


def left_right(left, right):
    lane = lax.broadcasted_iota(jnp.int32, left.shape, left.ndim - 1)
    return jnp.where(lane < left.shape[-1] // 2, left, right)


def first_kernel(
    pos_ref, v_any, b_any, c_any, p_any, near_any, count_any, leaf_any, t_any, ids_any,
    out_ref, up_ref, near_idx, leaf_idx, c0_ref, c1_ref, c2_ref, c3_ref,
    v, b, c, p, near, count, leaf, t, ids, mid, sems, *, total,
):
    copies = load(
        (near_any, count_any, leaf_any, t_any, ids_any, v_any, b_any, c_any, p_any),
        (near, count, leaf, t, ids, v, b, c, p),
        sems,
    )
    n, _, k = b.shape
    cols = v.shape[2]
    half = n // 2
    rank = pos_ref[1]
    piece = k // 4

    slots = near.shape[0]
    own_first = pos_ref[0] * n
    side = pos_ref[2]
    leaf_ids = own_first + lax.broadcasted_iota(jnp.int32, near.shape, 1)

    def place(offsets):
        rel = jnp.clip(leaf_ids + offsets, 0, total - 1) - own_first
        under = rel + jnp.where(side == 0, 2 * n, 3 * n)
        over = rel + jnp.where(side == 0, n, 0)
        return jnp.where(rel < 0, under, jnp.where(rel >= n, over, rel))

    slot = rank * slots + lax.broadcasted_iota(jnp.int32, near.shape, 0)
    for copy in copies[:5]:
        copy.wait()
    near_idx[...] = jnp.where(slot < count[...], place(near[...]), 3 * n)
    leaf_idx[...] = place(leaf[...])

    top_slots = t.shape[0]
    columns = []
    for r in range(4):
        part = jnp.concatenate([t[s, :, piece * r : piece * (r + 1)] for s in range(top_slots)], axis=1)
        columns.append(jnp.concatenate([part[: k // 2], part[k // 2 :]], axis=1))
    lane = lax.broadcasted_iota(jnp.int32, (16, 2 * k), 1)
    row = jnp.zeros((16, 2 * k), F32)
    for s in range(top_slots):
        row = jnp.where(lane == s, ids[0, s].astype(F32), row)
    for bit, ref in enumerate((c0_ref, c1_ref, c2_ref, c3_ref)):
        to = rank ^ bit
        part = columns[0]
        for r in range(1, 4):
            part = jnp.where(to == r, columns[r], part)
        ref[: k // 2] = part
        ref[k // 2 :] = row.astype(BF16)

    copies[5].wait()
    out_ref[:half] = jnp.concatenate([v[:half], v[half:]], axis=-1)
    copies[6].wait()
    for i in range(half):
        both = dot_t(jnp.concatenate([b[i], b[half + i]], axis=1), out_ref[i])
        out_ref[half + i] = left_right(both[:k], both[k:]).astype(BF16)
    copies[7].wait()
    for m in range(n // 16):
        here = out_ref[half + 8 * m : half + 8 * m + 8].reshape(8 * k, 2 * cols)
        low = dot_t(c[8 * m : 8 * m + 8].reshape(8 * k, k), here)
        high = dot_t(c[half + 8 * m : half + 8 * m + 8].reshape(8 * k, k), here)
        mid[m] = left_right(low, high).astype(BF16)
    copies[8].wait()
    mids = n // 16
    here = mid[...].reshape(mids * k, 2 * cols)
    low = dot_t(p[:mids].reshape(mids * k, k), here)
    high = dot_t(p[mids:].reshape(mids * k, k), here)
    up = low[:, :cols] + high[:, cols:]
    quarter = up[:piece]
    for r in range(1, 4):
        quarter = jnp.where(rank == r, up[piece * r : piece * (r + 1)], quarter)
    quarter = jnp.concatenate([quarter[: piece // 2], quarter[piece // 2 :]], axis=-1).astype(BF16)
    for i in range(up_ref.shape[0]):
        up_ref[i] = quarter


def first(pos, vectors, basis, child, parent, near_offsets, near_count, leaf_offsets, coupling, ids, total):
    n, p, c = vectors.shape
    k = basis.shape[2]
    sources = (vectors, basis, child, parent)
    small = (near_offsets, near_count, leaf_offsets)
    shape = near_offsets.shape
    return pl.pallas_call(
        functools.partial(first_kernel, total=total),
        out_shape=(
            jax.ShapeDtypeStruct((n, p, 2 * c), BF16),
            jax.ShapeDtypeStruct((total // n, k // 8, 2 * c), BF16),
            jax.ShapeDtypeStruct(shape, jnp.int32),
            jax.ShapeDtypeStruct(shape, jnp.int32),
        )
        + (jax.ShapeDtypeStruct((k // 2 + 16, 2 * k), BF16),) * 4,
        in_specs=[SMEM] + [pl.BlockSpec(memory_space=pltpu.HBM)] * 9,
        out_specs=(VMEM,) * 8,
        scratch_shapes=[pltpu.VMEM(a.shape, BF16) for a in sources]
        + [
            pltpu.VMEM(shape, jnp.int32),
            pltpu.VMEM(near_count.shape, jnp.int32),
            pltpu.VMEM(shape, jnp.int32),
            pltpu.VMEM(coupling.shape, BF16),
            pltpu.SMEM(ids.shape, jnp.int32),
            pltpu.VMEM((n // 16, k, 2 * c), BF16),
            pltpu.SemaphoreType.DMA((9,)),
        ],
        compiler_params=params(16),
        cost_estimate=cost(3.0),
        name="first",
    )(pos, *pinned(*sources, *small, coupling, ids))


CHUNK = 8
AHEAD = 3


def fields_kernel(
    near_idx, leaf_idx, own_ref, a_ref, b_ref, near_any, leaf_any, near_out, leaf_out, near, leaf, vec, mom, sems
):
    n, slots, p, k = near.shape
    chunks = n // CHUNK
    parts = []
    for i in range(chunks):
        rows = pl.ds(i * CHUNK, CHUNK)
        parts.append(
            [
                pltpu.make_async_copy(src.at[rows], dst.at[rows], sems.at[2 * i + j])
                for j, (src, dst) in enumerate(((near_any, near), (leaf_any, leaf)))
            ]
        )
    for i in range(AHEAD):
        for c in parts[i]:
            c.start()
    half = n // 2
    cols = own_ref.shape[2] // 2
    for i, ref in enumerate((own_ref, a_ref, b_ref)):
        for to, first in ((vec, 0), (mom, half)):
            to[n * i : n * i + half] = ref[first : first + half, :, :cols]
            to[n * i + half : n * (i + 1)] = ref[first : first + half, :, cols:]
    vec[3 * n] = jnp.zeros(vec.shape[1:], BF16)

    for i in range(chunks):
        for c in parts[i]:
            c.wait()
        if i + AHEAD < chunks:
            for c in parts[i + AHEAD]:
                c.start()
        for blocks, idx, store, out in ((near, near_idx, vec, near_out), (leaf, leaf_idx, mom, leaf_out)):
            for l in range(i * CHUNK, (i + 1) * CHUNK):
                total = None
                for g in range(0, slots, 4):
                    lhs = jnp.concatenate([blocks[l, g + j] for j in range(4)], axis=1)
                    rhs = jnp.concatenate([store[idx[g + j, l]] for j in range(4)], axis=0)
                    term = dot(lhs, rhs)
                    total = term if total is None else total + term
                out[l] = total


def fields(near_idx, leaf_idx, own, a, b, near, leaf):
    n, slots, p, k = near.shape
    c = own.shape[2] // 2
    out = jax.ShapeDtypeStruct((n, p, c), F32)
    return pl.pallas_call(
        fields_kernel,
        out_shape=(out, out),
        in_specs=[SMEM] * 2 + [VMEM] * 3 + [pl.BlockSpec(memory_space=pltpu.HBM)] * 2,
        out_specs=(VMEM, VMEM),
        scratch_shapes=[
            pltpu.VMEM(near.shape, BF16),
            pltpu.VMEM(leaf.shape, BF16),
            pltpu.VMEM((3 * n + 1, p, c), BF16),
            pltpu.VMEM((3 * n, k, c), BF16),
            pltpu.SemaphoreType.DMA((2 * n // CHUNK,)),
        ],
        compiler_params=params(26),
        cost_estimate=cost(8.0),
        name="fields",
    )(near_idx, leaf_idx, own, a, b, *pinned(near, leaf))


def join_kernel(
    pos_ref, up_ref, c0_ref, c1_ref, c2_ref, c3_ref, par_ref, leaf_ref, near_ref, child_ref, basis_ref,
    send_ref, keep_ref, mid, ids_v, ids_s, sem,
):
    cols = near_ref.shape[2]
    k = par_ref.shape[1]
    core = pos_ref[1] & 1
    parts = (c0_ref, c1_ref, c2_ref, c3_ref)
    ids_v[...] = jnp.zeros(ids_v.shape, jnp.int32)
    for b, ref in enumerate(parts):
        ids_v[b : b + 1] = ref[k // 2 :].astype(F32).astype(jnp.int32)[:1]
    copy = pltpu.make_async_copy(ids_v, ids_s, sem)
    copy.start()
    lhs = [ref[: k // 2] for ref in parts]
    lhs = jnp.concatenate([jnp.concatenate([c[:, :k], c[:, k:]], axis=0) for c in lhs], axis=1)
    copy.wait()
    rhs = []
    for b in range(4):
        for s in range(4):
            u = up_ref[ids_s[b, s]].astype(F32)
            rhs += [u[:, :cols], u[:, cols:]]
    top = dot(lhs, jnp.concatenate(rhs, axis=0).astype(BF16))
    top = top.astype(BF16)
    for m in range(par_ref.shape[0]):
        mid[m] = dot(par_ref[m], top).astype(BF16)

    rows = send_ref.shape[1]
    for l in range(near_ref.shape[0]):
        field = leaf_ref[l] + dot(child_ref[l], mid[l // 8])
        part = (near_ref[l] + dot(basis_ref[l], field.astype(BF16))).astype(BF16)
        quarter = [part[rows * i : rows * (i + 1)] for i in range(4)]
        even = jnp.concatenate([quarter[0], quarter[2]], axis=1)
        odd = jnp.concatenate([quarter[1], quarter[3]], axis=1)
        keep_ref[l] = jnp.where(core == 0, even, odd)
        send_ref[l] = jnp.where(core == 0, odd, even)


def join(pos, upper, coupling, parent, leaf_part, near_part, child, basis):
    n, p, c = near_part.shape
    k = parent.shape[1]
    out = jax.ShapeDtypeStruct((n, p // 4, 2 * c), BF16)
    return pl.pallas_call(
        join_kernel,
        out_shape=(out, out),
        in_specs=[SMEM] + [VMEM] * 10,
        out_specs=(VMEM, VMEM),
        scratch_shapes=[
            pltpu.VMEM((parent.shape[0], k, c), BF16),
            pltpu.VMEM((8, 2 * k), jnp.int32),
            pltpu.SMEM((8, 2 * k), jnp.int32),
            pltpu.SemaphoreType.DMA,
        ],
        compiler_params=params(8),
        cost_estimate=cost(2.0),
        name="join",
    )(pos, upper, *coupling, parent, leaf_part, near_part, child, basis)


def half_kernel(s_ref, keep_ref, recv_ref, send_ref, own_ref):
    c = keep_ref.shape[2] // 2
    n = keep_ref.shape[0]
    low = s_ref[0] == 0
    total = keep_ref[...].astype(F32) + recv_ref[...].astype(F32)
    first, second = total[:, :, :c], total[:, :, c:]
    own_ref[...] = jnp.where(low, first, second)
    other = jnp.where(low, second, first).astype(BF16)
    send_ref[...] = jnp.concatenate([other[: n // 2], other[n // 2 :]], axis=-1)


def half_sum(scalars, keep, recv):
    n, rows, c2 = keep.shape
    return pl.pallas_call(
        half_kernel,
        out_shape=(
            jax.ShapeDtypeStruct((n // 2, rows, c2), BF16),
            jax.ShapeDtypeStruct((n, rows, c2 // 2), F32),
        ),
        in_specs=[SMEM, VMEM, VMEM],
        out_specs=(VMEM, VMEM),
        compiler_params=params(8),
        cost_estimate=cost(0.3),
        name="half_sum",
    )(scalars, keep, recv)


def last_kernel(own_ref, recv_ref, out_ref):
    n = own_ref.shape[0]
    c = own_ref.shape[2]
    recv = recv_ref[...].astype(F32)
    out_ref[: n // 2] = (own_ref[: n // 2] + recv[:, :, :c]).astype(BF16)
    out_ref[n // 2 :] = (own_ref[n // 2 :] + recv[:, :, c:]).astype(BF16)


def last_sum(own, recv):
    return pl.pallas_call(
        last_kernel,
        out_shape=jax.ShapeDtypeStruct(own.shape, BF16),
        in_specs=[VMEM, VMEM],
        out_specs=VMEM,
        compiler_params=params(8),
        cost_estimate=cost(0.5),
        name="last_sum",
    )(own, recv)


AXES = ("leaf", "rank")


def halo_pairs(leaves):
    out = []
    for leaf in range(leaves):
        for rank in range(4):
            high = (rank & 1) != (leaf >= leaves // 2)
            to = leaf + 1 if high else leaf - 1
            if 0 <= to < leaves:
                cross = {leaf, to} == {leaves // 2 - 1, leaves // 2}
                out.append((leaf * 4 + rank, to * 4 + (rank ^ (2 if cross else 1))))
    return out


def shards(
    vectors,
    near_blocks,
    near_offsets,
    near_count,
    basis,
    child_transfer,
    parent_transfer,
    leaf_coupling,
    leaf_offsets,
    top_coupling,
    top_ids,
):
    leaf_dev, points, columns = vectors.shape
    leaves = lax.axis_size("leaf")
    total_leaves = leaf_dev * leaves
    leaf_pos = lax.axis_index("leaf")
    rank_pos = lax.axis_index("rank")
    core = rank_pos % 2
    y_lo = rank_pos // 2
    side = core ^ (leaf_pos >= leaves // 2)
    pos = jnp.stack([leaf_pos, rank_pos, side]).astype(jnp.int32)

    route = halo_pairs(leaves)
    swap = [(i, i ^ 1) for i in range(4)]
    own, upper, near_idx, leaf_idx, *coupling = first(
        pos,
        vectors,
        basis,
        child_transfer,
        parent_transfer,
        near_offsets.T,
        near_count[None],
        leaf_offsets.T,
        top_coupling[0],
        top_ids,
        total_leaves,
    )
    halo_a = lax.ppermute(own, AXES, route)
    upper = lax.all_to_all(upper, "leaf", 0, 0)
    halo_a, upper, coupling = lax.optimization_barrier((halo_a, upper, coupling))
    halo_b = lax.ppermute(halo_a, "rank", swap)
    coupling = coupling[:1] + [
        lax.ppermute(coupling[bit], "rank", [(i, i ^ bit) for i in range(4)]) for bit in (1, 2, 3)
    ]
    near_part, leaf_part = fields(near_idx, leaf_idx, own, halo_a, halo_b, near_blocks, leaf_coupling)
    send, keep = join(
        pos, upper, coupling, parent_transfer, leaf_part, near_part, child_transfer, basis
    )
    recv = lax.ppermute(send, "rank", swap)
    send, own = half_sum(y_lo[None].astype(jnp.int32), keep, recv)
    recv = lax.ppermute(send, "rank", [(i, i ^ 2) for i in range(4)])
    return last_sum(own, recv)


def solution(mesh):
    in_specs = (
        P("leaf", None, None),
        P("leaf", "rank", None, None),
        P("leaf", "rank"),
        P("leaf"),
        P("leaf", None, None),
        P("leaf", None, None),
        P("leaf", None, None),
        P("leaf", "rank", None, None),
        P("leaf", "rank"),
        P("leaf", "rank", None, None),
        P("leaf", "rank"),
    )
    out_specs = P("leaf", "rank", None)
    return jax.shard_map(shards, mesh=mesh, in_specs=in_specs, out_specs=out_specs, check_vma=False)
```

```python
import functools

import jax
import jax.numpy as jnp
from jax import lax
from jax.experimental import pallas as pl
from jax.experimental.pallas import tpu as pltpu
from jax.sharding import PartitionSpec as P

F32 = jnp.float32
BF16 = jnp.bfloat16
MIB = 1024 * 1024
VMEM = pl.BlockSpec(memory_space=pltpu.VMEM)
SMEM = pl.BlockSpec(memory_space=pltpu.SMEM)


def params(mib):
    return pltpu.CompilerParams(vmem_limit_bytes=mib * MIB)


def cost(us):
    return pl.CostEstimate(flops=0, bytes_accessed=int(us * 3.0e6), transcendentals=0)


def dot(a, b):
    return jnp.dot(a, b, preferred_element_type=F32)


def dot_t(a, b):
    return lax.dot_general(a, b, (((0,), (0,)), ((), ())), preferred_element_type=F32)


def pinned(*arrays):
    return [pltpu.with_memory_space_constraint(a, pltpu.HBM) for a in arrays]


def load(sources, targets, sems):
    copies = [pltpu.make_async_copy(a, b, sems.at[i]) for i, (a, b) in enumerate(zip(sources, targets))]
    for copy in copies:
        copy.start()
    return copies


def left_right(left, right):
    lane = lax.broadcasted_iota(jnp.int32, left.shape, left.ndim - 1)
    return jnp.where(lane < left.shape[-1] // 2, left, right)


def first_kernel(
    pos_ref, v_any, b_any, c_any, p_any, near_any, count_any, leaf_any, t_any, ids_any,
    out_ref, up_ref, near_idx, leaf_idx, c0_ref, c1_ref, c2_ref, c3_ref,
    v, b, c, p, near, count, leaf, t, ids, mid, sems, *, total,
):
    copies = load(
        (near_any, count_any, leaf_any, t_any, ids_any, v_any, b_any, c_any, p_any),
        (near, count, leaf, t, ids, v, b, c, p),
        sems,
    )
    n, _, k = b.shape
    cols = v.shape[2]
    half = n // 2
    rank = pos_ref[1]
    piece = k // 4

    slots = near.shape[0]
    own_first = pos_ref[0] * n
    side = pos_ref[2]
    leaf_ids = own_first + lax.broadcasted_iota(jnp.int32, near.shape, 1)

    def place(offsets):
        rel = jnp.clip(leaf_ids + offsets, 0, total - 1) - own_first
        under = rel + jnp.where(side == 0, 2 * n, 3 * n)
        over = rel + jnp.where(side == 0, n, 0)
        return jnp.where(rel < 0, under, jnp.where(rel >= n, over, rel))

    slot = rank * slots + lax.broadcasted_iota(jnp.int32, near.shape, 0)
    for copy in copies[:5]:
        copy.wait()
    near_idx[...] = jnp.where(slot < count[...], place(near[...]), 3 * n)
    leaf_idx[...] = place(leaf[...])

    top_slots = t.shape[0]
    columns = []
    for r in range(4):
        part = jnp.concatenate([t[s, :, piece * r : piece * (r + 1)] for s in range(top_slots)], axis=1)
        columns.append(jnp.concatenate([part[: k // 2], part[k // 2 :]], axis=1))
    lane = lax.broadcasted_iota(jnp.int32, (16, 2 * k), 1)
    row = jnp.zeros((16, 2 * k), F32)
    for s in range(top_slots):
        row = jnp.where(lane == s, ids[0, s].astype(F32), row)
    for bit, ref in enumerate((c0_ref, c1_ref, c2_ref, c3_ref)):
        to = rank ^ bit
        part = columns[0]
        for r in range(1, 4):
            part = jnp.where(to == r, columns[r], part)
        ref[: k // 2] = part
        ref[k // 2 :] = row.astype(BF16)

    copies[5].wait()
    out_ref[:half] = jnp.concatenate([v[:half], v[half:]], axis=-1)
    copies[6].wait()
    for i in range(half):
        both = dot_t(jnp.concatenate([b[i], b[half + i]], axis=1), out_ref[i])
        out_ref[half + i] = left_right(both[:k], both[k:]).astype(BF16)
    copies[7].wait()
    for m in range(n // 16):
        here = out_ref[half + 8 * m : half + 8 * m + 8].reshape(8 * k, 2 * cols)
        low = dot_t(c[8 * m : 8 * m + 8].reshape(8 * k, k), here)
        high = dot_t(c[half + 8 * m : half + 8 * m + 8].reshape(8 * k, k), here)
        mid[m] = left_right(low, high).astype(BF16)
    copies[8].wait()
    mids = n // 16
    here = mid[...].reshape(mids * k, 2 * cols)
    low = dot_t(p[:mids].reshape(mids * k, k), here)
    high = dot_t(p[mids:].reshape(mids * k, k), here)
    up = low[:, :cols] + high[:, cols:]
    quarter = up[:piece]
    for r in range(1, 4):
        quarter = jnp.where(rank == r, up[piece * r : piece * (r + 1)], quarter)
    quarter = jnp.concatenate([quarter[: piece // 2], quarter[piece // 2 :]], axis=-1).astype(BF16)
    for i in range(up_ref.shape[0]):
        up_ref[i] = quarter


def first(pos, vectors, basis, child, parent, near_offsets, near_count, leaf_offsets, coupling, ids, total):
    n, p, c = vectors.shape
    k = basis.shape[2]
    sources = (vectors, basis, child, parent)
    small = (near_offsets, near_count, leaf_offsets)
    shape = near_offsets.shape
    return pl.pallas_call(
        functools.partial(first_kernel, total=total),
        out_shape=(
            jax.ShapeDtypeStruct((n, p, 2 * c), BF16),
            jax.ShapeDtypeStruct((total // n, k // 8, 2 * c), BF16),
            jax.ShapeDtypeStruct(shape, jnp.int32),
            jax.ShapeDtypeStruct(shape, jnp.int32),
        )
        + (jax.ShapeDtypeStruct((k // 2 + 16, 2 * k), BF16),) * 4,
        in_specs=[SMEM] + [pl.BlockSpec(memory_space=pltpu.HBM)] * 9,
        out_specs=(VMEM,) * 8,
        scratch_shapes=[pltpu.VMEM(a.shape, BF16) for a in sources]
        + [
            pltpu.VMEM(shape, jnp.int32),
            pltpu.VMEM(near_count.shape, jnp.int32),
            pltpu.VMEM(shape, jnp.int32),
            pltpu.VMEM(coupling.shape, BF16),
            pltpu.SMEM(ids.shape, jnp.int32),
            pltpu.VMEM((n // 16, k, 2 * c), BF16),
            pltpu.SemaphoreType.DMA((9,)),
        ],
        compiler_params=params(16),
        cost_estimate=cost(3.0),
        name="first",
    )(pos, *pinned(*sources, *small, coupling, ids))


CHUNK = 8
AHEAD = 2


def fields_kernel(
    near_idx, leaf_idx, own_ref, a_ref, b_ref, near_any, leaf_any, near_out, leaf_out, near, leaf, vec, mom, sems
):
    n, slots, p, k = near.shape
    chunks = n // CHUNK
    parts = []
    for i in range(chunks):
        rows = pl.ds(i * CHUNK, CHUNK)
        parts.append(
            [
                pltpu.make_async_copy(src.at[rows], dst.at[rows], sems.at[2 * i + j])
                for j, (src, dst) in enumerate(((near_any, near), (leaf_any, leaf)))
            ]
        )
    for i in range(AHEAD):
        for c in parts[i]:
            c.start()
    half = n // 2
    cols = own_ref.shape[2] // 2
    for i, ref in enumerate((own_ref, a_ref, b_ref)):
        for to, first in ((vec, 0), (mom, half)):
            to[n * i : n * i + half] = ref[first : first + half, :, :cols]
            to[n * i + half : n * (i + 1)] = ref[first : first + half, :, cols:]
    vec[3 * n] = jnp.zeros(vec.shape[1:], BF16)

    for i in range(chunks):
        for c in parts[i]:
            c.wait()
        if i + AHEAD < chunks:
            for c in parts[i + AHEAD]:
                c.start()
        for blocks, idx, store, out in ((near, near_idx, vec, near_out), (leaf, leaf_idx, mom, leaf_out)):
            for l in range(i * CHUNK, (i + 1) * CHUNK):
                total = None
                for g in range(0, slots, 4):
                    lhs = jnp.concatenate([blocks[l, g + j] for j in range(4)], axis=1)
                    rhs = jnp.concatenate([store[idx[g + j, l]] for j in range(4)], axis=0)
                    term = dot(lhs, rhs)
                    total = term if total is None else total + term
                out[l] = total


def fields(near_idx, leaf_idx, own, a, b, near, leaf):
    n, slots, p, k = near.shape
    c = own.shape[2] // 2
    out = jax.ShapeDtypeStruct((n, p, c), F32)
    return pl.pallas_call(
        fields_kernel,
        out_shape=(out, out),
        in_specs=[SMEM] * 2 + [VMEM] * 3 + [pl.BlockSpec(memory_space=pltpu.HBM)] * 2,
        out_specs=(VMEM, VMEM),
        scratch_shapes=[
            pltpu.VMEM(near.shape, BF16),
            pltpu.VMEM(leaf.shape, BF16),
            pltpu.VMEM((3 * n + 1, p, c), BF16),
            pltpu.VMEM((3 * n, k, c), BF16),
            pltpu.SemaphoreType.DMA((2 * n // CHUNK,)),
        ],
        compiler_params=params(26),
        cost_estimate=cost(8.0),
        name="fields",
    )(near_idx, leaf_idx, own, a, b, *pinned(near, leaf))


def join_kernel(
    pos_ref, up_ref, c0_ref, c1_ref, c2_ref, c3_ref, par_ref, leaf_ref, near_ref, child_ref, basis_ref,
    send_ref, keep_ref, mid, ids_v, ids_s, sem,
):
    cols = near_ref.shape[2]
    k = par_ref.shape[1]
    core = pos_ref[1] & 1
    parts = (c0_ref, c1_ref, c2_ref, c3_ref)
    ids_v[...] = jnp.zeros(ids_v.shape, jnp.int32)
    for b, ref in enumerate(parts):
        ids_v[b : b + 1] = ref[k // 2 :].astype(F32).astype(jnp.int32)[:1]
    copy = pltpu.make_async_copy(ids_v, ids_s, sem)
    copy.start()
    lhs = [ref[: k // 2] for ref in parts]
    lhs = jnp.concatenate([jnp.concatenate([c[:, :k], c[:, k:]], axis=0) for c in lhs], axis=1)
    copy.wait()
    rhs = []
    for b in range(4):
        for s in range(4):
            u = up_ref[ids_s[b, s]].astype(F32)
            rhs += [u[:, :cols], u[:, cols:]]
    top = dot(lhs, jnp.concatenate(rhs, axis=0).astype(BF16))
    top = top.astype(BF16)
    for m in range(par_ref.shape[0]):
        mid[m] = dot(par_ref[m], top).astype(BF16)

    rows = send_ref.shape[1]
    for l in range(near_ref.shape[0]):
        field = leaf_ref[l] + dot(child_ref[l], mid[l // 8])
        part = (near_ref[l] + dot(basis_ref[l], field.astype(BF16))).astype(BF16)
        quarter = [part[rows * i : rows * (i + 1)] for i in range(4)]
        even = jnp.concatenate([quarter[0], quarter[2]], axis=1)
        odd = jnp.concatenate([quarter[1], quarter[3]], axis=1)
        keep_ref[l] = jnp.where(core == 0, even, odd)
        send_ref[l] = jnp.where(core == 0, odd, even)


def join(pos, upper, coupling, parent, leaf_part, near_part, child, basis):
    n, p, c = near_part.shape
    k = parent.shape[1]
    out = jax.ShapeDtypeStruct((n, p // 4, 2 * c), BF16)
    return pl.pallas_call(
        join_kernel,
        out_shape=(out, out),
        in_specs=[SMEM] + [VMEM] * 10,
        out_specs=(VMEM, VMEM),
        scratch_shapes=[
            pltpu.VMEM((parent.shape[0], k, c), BF16),
            pltpu.VMEM((8, 2 * k), jnp.int32),
            pltpu.SMEM((8, 2 * k), jnp.int32),
            pltpu.SemaphoreType.DMA,
        ],
        compiler_params=params(8),
        cost_estimate=cost(2.0),
        name="join",
    )(pos, upper, *coupling, parent, leaf_part, near_part, child, basis)


def half_kernel(s_ref, keep_ref, recv_ref, send_ref, own_ref):
    c = keep_ref.shape[2] // 2
    n = keep_ref.shape[0]
    low = s_ref[0] == 0
    total = keep_ref[...].astype(F32) + recv_ref[...].astype(F32)
    first, second = total[:, :, :c], total[:, :, c:]
    own_ref[...] = jnp.where(low, first, second)
    other = jnp.where(low, second, first).astype(BF16)
    send_ref[...] = jnp.concatenate([other[: n // 2], other[n // 2 :]], axis=-1)


def half_sum(scalars, keep, recv):
    n, rows, c2 = keep.shape
    return pl.pallas_call(
        half_kernel,
        out_shape=(
            jax.ShapeDtypeStruct((n // 2, rows, c2), BF16),
            jax.ShapeDtypeStruct((n, rows, c2 // 2), F32),
        ),
        in_specs=[SMEM, VMEM, VMEM],
        out_specs=(VMEM, VMEM),
        compiler_params=params(8),
        cost_estimate=cost(0.3),
        name="half_sum",
    )(scalars, keep, recv)


def last_kernel(own_ref, recv_ref, out_ref):
    n = own_ref.shape[0]
    c = own_ref.shape[2]
    recv = recv_ref[...].astype(F32)
    out_ref[: n // 2] = (own_ref[: n // 2] + recv[:, :, :c]).astype(BF16)
    out_ref[n // 2 :] = (own_ref[n // 2 :] + recv[:, :, c:]).astype(BF16)


def last_sum(own, recv):
    return pl.pallas_call(
        last_kernel,
        out_shape=jax.ShapeDtypeStruct(own.shape, BF16),
        in_specs=[VMEM, VMEM],
        out_specs=VMEM,
        compiler_params=params(8),
        cost_estimate=cost(0.5),
        name="last_sum",
    )(own, recv)


AXES = ("leaf", "rank")


def halo_pairs(leaves):
    out = []
    for leaf in range(leaves):
        for rank in range(4):
            high = (rank & 1) != (leaf >= leaves // 2)
            to = leaf + 1 if high else leaf - 1
            if 0 <= to < leaves:
                cross = {leaf, to} == {leaves // 2 - 1, leaves // 2}
                out.append((leaf * 4 + rank, to * 4 + (rank ^ (2 if cross else 1))))
    return out


def shards(
    vectors,
    near_blocks,
    near_offsets,
    near_count,
    basis,
    child_transfer,
    parent_transfer,
    leaf_coupling,
    leaf_offsets,
    top_coupling,
    top_ids,
):
    leaf_dev, points, columns = vectors.shape
    leaves = lax.axis_size("leaf")
    total_leaves = leaf_dev * leaves
    leaf_pos = lax.axis_index("leaf")
    rank_pos = lax.axis_index("rank")
    core = rank_pos % 2
    y_lo = rank_pos // 2
    side = core ^ (leaf_pos >= leaves // 2)
    pos = jnp.stack([leaf_pos, rank_pos, side]).astype(jnp.int32)

    route = halo_pairs(leaves)
    swap = [(i, i ^ 1) for i in range(4)]
    own, upper, near_idx, leaf_idx, *coupling = first(
        pos,
        vectors,
        basis,
        child_transfer,
        parent_transfer,
        near_offsets.T,
        near_count[None],
        leaf_offsets.T,
        top_coupling[0],
        top_ids,
        total_leaves,
    )
    halo_a = lax.ppermute(own, AXES, route)
    upper = lax.all_to_all(upper, "leaf", 0, 0)
    halo_a, upper, coupling = lax.optimization_barrier((halo_a, upper, coupling))
    halo_b = lax.ppermute(halo_a, "rank", swap)
    coupling = coupling[:1] + [
        lax.ppermute(coupling[bit], "rank", [(i, i ^ bit) for i in range(4)]) for bit in (1, 2, 3)
    ]
    near_part, leaf_part = fields(near_idx, leaf_idx, own, halo_a, halo_b, near_blocks, leaf_coupling)
    send, keep = join(
        pos, upper, coupling, parent_transfer, leaf_part, near_part, child_transfer, basis
    )
    recv = lax.ppermute(send, "rank", swap)
    send, own = half_sum(y_lo[None].astype(jnp.int32), keep, recv)
    recv = lax.ppermute(send, "rank", [(i, i ^ 2) for i in range(4)])
    return last_sum(own, recv)


def solution(mesh):
    in_specs = (
        P("leaf", None, None),
        P("leaf", "rank", None, None),
        P("leaf", "rank"),
        P("leaf"),
        P("leaf", None, None),
        P("leaf", None, None),
        P("leaf", None, None),
        P("leaf", "rank", None, None),
        P("leaf", "rank"),
        P("leaf", "rank", None, None),
        P("leaf", "rank"),
    )
    out_specs = P("leaf", "rank", None)
    return jax.shard_map(shards, mesh=mesh, in_specs=in_specs, out_specs=out_specs, check_vma=False)
```
